32 devices in a mesh: space: 8 (over y, x, core), band: 4 (over z).
Axes of the slice: x: 2, y: 2, z: 4, core: 2. Of those that a mesh axis runs over, the one named last changes fastest.
Arguments:
- states_in: bfloat16 [256, 16384], P('band', 'space'), may hold values from -6 to 6
- kinetic: bfloat16 [64, 64], replicated, may hold values from -0.75 to 0.75
- cell_scale: float32 [2048], P('space'), may hold values from 0.5 to 2
- cell_nodes: int32 [64, 2048], P(None, 'space'), may hold values from 0 to 4095
- boundary: int32 [4096], P('space'), may hold values from 0 to 2047, as said below
- potential: float32 [16384], P('space'), may hold values from -2 to 2
- inv_mass_root: float32 [16384], P('space'), may hold values from 0.2 to 1.875
Outputs:
- filtered: bfloat16 [256, 16384], P('band', 'space')
- margin: float32 [256, 256], P('band')
The draws below stay inside these ranges and needn't reach their ends.
Inputs may be any that keep to these rules, and one draw needn't show every extreme that they name: `boundary`: each partition's 512 entries are distinct node numbers of that partition. `cell_nodes`: A value below 2048 is a node of the cell's own partition; a value 2048 + j * 512 + b is entry b of the boundary list of the partition whose space index is the cell's own plus (-2, -1, 1, 2)[j], taken modulo the number of partitions.
All inputs are finite; a program needn't handle non-finite values.
Results may differ from the reference program's by a relative error of at most 0.0095.
Values may be sent and summed in bfloat16 or wider, within the bound.
A program may use at most 64 MiB of HBM per device.

```python
import math
import jax
import jax.numpy as jnp
from jax import lax

STATES = 256
CELL_NODES = 64
N_DEV = 2048
C_DEV = 256
NB = 512
NODES = 16384
CELLS = 2048
N_SPACE = 8
N_BAND = 4


def draw_boundary(key, part):
    keys = jax.random.split(jax.random.fold_in(key, 11), N_SPACE)
    lists = jax.vmap(lambda single: jax.random.permutation(single, N_DEV)[:NB])(keys)
    return lists.reshape(-1).astype(jnp.int32)


def draw_inv_mass_root(key, part):
    position = jnp.arange(NODES, dtype=jnp.float32) / NODES
    rough = jnp.exp(jax.random.uniform(jax.random.fold_in(key, 23), (NODES,), jnp.float32, jnp.log(0.8), jnp.log(1.25)))
    grade = 0.4 * jnp.power(3.0, position)
    return (grade * rough).astype(jnp.float32)


def place_ends(result, key, least, largest):
    longest = result.shape.index(max(result.shape))
    spots = []
    for shift in (0, 1):
        where = [jax.random.randint(jax.random.fold_in(key, axis), (), 0, length) for axis, length in enumerate(result.shape)]
        where[longest] = (where[longest] + shift) % result.shape[longest]
        spots.append(tuple(where))
    return result.at[spots[0]].set(least).at[spots[1]].set(largest)


def shard_levels(rng, extent, cuts, least, top_value):
    factor_of = 1.0
    for axis_at, shards_of in cuts:
        heights = jax.random.uniform(jax.random.fold_in(jax.random.fold_in(rng, 6), axis_at), (shards_of,), jnp.float32, least / len(cuts), top_value / len(cuts))
        factor_of = factor_of * jnp.repeat(jnp.exp(heights), extent[axis_at] // shards_of).reshape((-1,) + (1,) * (len(extent) - 1 - axis_at))
    return factor_of


def noise(stream_key, extent, deviation, limit, cuts=(), held_as=jnp.bfloat16):
    factor_of = shard_levels(stream_key, extent, cuts, -0.22, 0.18) if cuts else 1.0
    result = jax.random.normal(stream_key, extent, jnp.float32) * deviation * factor_of
    return jnp.minimum(jnp.maximum(result, -limit), limit).astype(held_as)


def setup_inputs(seed: int = 0) -> dict:
    streams_of = jax.random.split(jax.random.key(seed), 8)
    return {
        "states_in": noise(streams_of[0], (STATES, NODES), 1.0, 6.0, ((0, 4), (1, 8))),
        "kinetic": noise(streams_of[1], (CELL_NODES, CELL_NODES), CELL_NODES ** -0.5, 0.75),
        "cell_scale": jnp.clip(jnp.exp(math.log(2.0) - 1.3862944 * jax.random.uniform(streams_of[2], (CELLS,), jnp.float32) ** shard_levels(streams_of[2], (CELLS,), ((0, 8),), -0.2, 0.2)), 0.5, 2.0),
        "cell_nodes": place_ends(jax.random.randint(streams_of[3], (CELL_NODES, CELLS), 0, N_DEV + 4 * NB), jax.random.fold_in(streams_of[3], 1), 0, (N_DEV + 4 * NB) - 1).astype(jnp.int32),
        "boundary": draw_boundary(jax.random.fold_in(streams_of[7], 71), 0),
        "potential": jnp.clip(jax.random.uniform(streams_of[5], (NODES,), jnp.float32, -2.0, 2.0) * shard_levels(streams_of[5], (NODES,), ((0, 8),), -0.4, 0.0), -2.0, 2.0),
        "inv_mass_root": draw_inv_mass_root(jax.random.fold_in(streams_of[7], 71), 0),
    }


OFFSETS = (-2, -1, 1, 2)
CENTER = 0.5
HALF = 6.0


def global_ids(cell_nodes, boundary):
    cell_count = cell_nodes.shape[1]
    owner = (jnp.arange(cell_count, dtype=jnp.int32) // C_DEV).astype(jnp.int32)[None, :]
    ghost = jnp.maximum(cell_nodes - N_DEV, 0)
    slot_index = ghost // NB
    entry = ghost % NB
    shifts = jnp.array(OFFSETS, dtype=jnp.int32)[slot_index]
    source = (owner + shifts) % N_SPACE
    remote = source * N_DEV + boundary[source * NB + entry]
    return jnp.where(cell_nodes < N_DEV, owner * N_DEV + cell_nodes, remote).astype(jnp.int32)


def apply_operator(values, kinetic, id_blocks, scale_blocks, potential, inv_root):
    width = values.shape[1]
    scaled = (inv_root[:, None] * values.astype(jnp.float32)).astype(jnp.bfloat16)
    kinetic_f = kinetic.astype(jnp.float32)

    def add_cells(totals, item):
        indices, scales_here = item
        gathered = scaled[indices].astype(jnp.float32)
        terms = jnp.einsum('ij,jcs->ics', kinetic_f, gathered) * scales_here[None, :, None]
        totals = totals.at[indices.reshape(-1)].add(terms.reshape(-1, width))
        return totals, None

    totals = lax.scan(add_cells, jnp.zeros((values.shape[0], width), jnp.float32), (id_blocks, scale_blocks))[0]
    return inv_root[:, None] * (totals + potential[:, None] * scaled.astype(jnp.float32))


def reference(states_in, kinetic, cell_scale, cell_nodes, boundary, potential, inv_mass_root):
    ids = global_ids(cell_nodes, boundary)
    id_blocks = ids.reshape(CELL_NODES, N_SPACE, C_DEV).transpose(1, 0, 2)
    scale_blocks = cell_scale.reshape(N_SPACE, C_DEV)
    block_rows = STATES // N_BAND
    seconds = []
    outputs = []
    for block in range(N_BAND):
        start_v = states_in[block * block_rows:(block + 1) * block_rows].T
        image = apply_operator(start_v, kinetic, id_blocks, scale_blocks, potential, inv_mass_root)
        first = ((image - CENTER * start_v.astype(jnp.float32)) / HALF).astype(jnp.bfloat16)
        image_two = apply_operator(first, kinetic, id_blocks, scale_blocks, potential, inv_mass_root)
        second = 2.0 * (image_two - CENTER * first.astype(jnp.float32)) / HALF - start_v.astype(jnp.float32)
        seconds.append(second.T)
        outputs.append(second.T.astype(jnp.bfloat16))
    filtered = jnp.concatenate(outputs, axis=0)
    rows_list = []
    for left in seconds:
        pieces = [lax.dot_general(left, right, (((1,), (1,)), ((), ())), precision=lax.Precision.HIGHEST, preferred_element_type=jnp.float32) for right in seconds]
        rows_list.append(jnp.concatenate(pieces, axis=1))
    margin = jnp.concatenate(rows_list, axis=0) / NODES
    return filtered, margin
```

```python
import functools

import jax
import jax.numpy as jnp
from jax import lax
from jax.experimental import pallas as pl
from jax.experimental.pallas import tpu as pltpu
from jax.sharding import PartitionSpec as P

OFFSETS = (-2, -1, 1, 2)
CENTER = 0.5
HALF = 6.0
LANES = 256
CHUNK = 16
F32 = jnp.float32
BF16 = jnp.bfloat16
NT = (((1,), (1,)), ((), ()))
VMEM = pl.BlockSpec(memory_space=pltpu.VMEM)


def from_behind(x, axis, by):
    count = lax.axis_size(axis)
    return lax.ppermute(x, axis, [(i, (i + by) % count) for i in range(count)])


def call(kernel, out_shape, *args, scratch=(), specs=None):
    return pl.pallas_call(
        kernel,
        out_shape=out_shape,
        in_specs=specs or [VMEM] * len(args),
        out_specs=jax.tree.map(lambda _: VMEM, out_shape),
        scratch_shapes=scratch,
        compiler_params=pltpu.CompilerParams(vmem_limit_bytes=56 * 2**20),
    )(*args)


def boundary_hot(boundary, nodes):
    shape = (nodes, boundary.shape[-1])
    return jnp.where(lax.broadcasted_iota(jnp.int32, shape, 0) == boundary, 1.0, 0.0).astype(BF16)


def scaled_of(values, inv_root):
    return (inv_root * values.astype(F32)).astype(BF16)


def pre_kernel(values, inv_root, boundary, scaled_out, rim_out):
    scaled = scaled_of(values[...], inv_root[...])
    scaled_out[...] = scaled
    hot = boundary_hot(boundary[...], scaled.shape[1])
    rim_out[...] = jnp.dot(scaled, hot, preferred_element_type=F32).astype(BF16)


def cells_kernel(scaled, g0, g1, g2, g3, nodes, nodes_row, scale, block, own_out, o0, o1, o2, o3, table, total):
    rows, owned = scaled.shape
    rim = g0.shape[1]
    parts = LANES // rows
    height = table.shape[1]
    shift = height.bit_length() - 1
    corners = nodes.shape[0]
    step = CHUNK * corners

    def place(at, width):
        return at // height * rows, at % height, min(width, height)

    for at in range(0, owned, height):
        row, col, width = place(at, owned)
        table[row : row + rows, col : col + width] = scaled[:, at : at + width]
    for slot, ghost in enumerate((g0, g1, g2, g3)):
        row, col, width = place(owned + slot * rim, rim)
        table[row : row + rows, col : col + width] = ghost[...]
    total[...] = jnp.zeros_like(total)
    weights = table[...]
    lane = lax.broadcasted_iota(jnp.int32, (corners, 128), 1)
    part_lane = lane // rows
    lane_b = lane.astype(F32).astype(BF16)

    def chunk(g, carry):
        base = g * CHUNK
        block_at = pl.multiple_of(base // 128 * 128, 128)
        ids = nodes[:, pl.ds(block_at, 128)]
        ids = pltpu.roll(ids, (128 - base % 128) % 128, axis=1)
        low = (ids & 127).astype(F32)
        high = ((ids >> 7) & (height // 128 - 1)).astype(F32)
        part = ids >> shift
        hots, masks = [], []
        for c in range(CHUNK):
            lo = jnp.broadcast_to(low[:, c : c + 1], (corners, 128)).astype(BF16)
            hi = jnp.broadcast_to(high[:, c : c + 1], (corners, 128)).astype(BF16)
            pt = jnp.broadcast_to(part[:, c : c + 1], (corners, 128))
            one = jnp.where(lo == lane_b, 1.0, 0.0).astype(BF16)
            hots.append(
                jnp.concatenate(
                    [jnp.where(hi == jnp.asarray(b, BF16), one, jnp.zeros_like(one)) for b in range(height // 128)],
                    axis=1,
                )
            )
            masks.append(
                jnp.concatenate([pt == part_lane + k * (128 // rows) for k in range(LANES // 128)], axis=1)
            )
        hot = jnp.concatenate(hots, axis=0)
        found = lax.dot_general(hot, weights, NT, preferred_element_type=F32)
        terms = []
        per = LANES // corners
        for q in range(0, CHUNK, per):
            picked = jnp.concatenate(
                [
                    jnp.where(masks[c], found[c * corners : (c + 1) * corners], 0.0).astype(BF16)
                    for c in range(q, q + per)
                ],
                axis=0,
            )
            term = jnp.dot(block[...], picked, preferred_element_type=F32)
            folded = term[:, :128]
            for k in range(128, LANES, 128):
                folded = folded + term[:, k : k + 128]
            spread = rows
            while spread < 128:
                folded = folded + pltpu.roll(folded, spread, axis=1)
                spread *= 2
            for c in range(q, q + per):
                mine = folded[(c - q) * corners : (c - q + 1) * corners] * scale[base + c]
                wide = jnp.concatenate([mine] * (LANES // 128), axis=1)
                terms.append(jnp.where(masks[c], wide, 0.0).astype(BF16))
        spread_terms = jnp.concatenate(terms, axis=0)
        row = (nodes_row[pl.ds(g, 1), :] & (height - 1))
        hot_t = jnp.where(
            lax.broadcasted_iota(jnp.int32, (height, step), 0) == row, 1.0, 0.0
        ).astype(BF16)
        total[...] += jnp.dot(hot_t, spread_terms, preferred_element_type=F32)
        return carry

    lax.fori_loop(0, nodes.shape[1] // CHUNK, chunk, 0)
    result = total[...].T
    for at in range(0, owned, height):
        row, col, width = place(at, owned)
        own_out[:, at : at + width] = result[row : row + rows, col : col + width]
    for slot, out in enumerate((o0, o1, o2, o3)):
        row, col, width = place(owned + slot * rim, rim)
        out[...] = result[row : row + rows, col : col + width].astype(out.dtype)


def gathered_total(own, arrived, hot, scaled, potential, inv_root):
    extra = sum(a[...].astype(F32) for a in arrived)
    added = lax.dot_general(extra.astype(BF16), hot, NT, preferred_element_type=F32)
    return inv_root * (own + added + potential * scaled.astype(F32))


def mid_kernel(values, scaled, own, a0, a1, a2, a3, potential, inv_root, boundary, first_out, scaled_out, rim_out):
    hot = boundary_hot(boundary[...], own.shape[1])
    image = gathered_total(own[...], (a0, a1, a2, a3), hot, scaled[...], potential[...], inv_root[...])
    first = ((image - CENTER * values[...].astype(F32)) * (1.0 / HALF)).astype(BF16)
    first_out[...] = first
    again = scaled_of(first, inv_root[...])
    scaled_out[...] = again
    rim_out[...] = jnp.dot(again, hot, preferred_element_type=F32).astype(BF16)


def post_kernel(start, first, scaled, own, a0, a1, a2, a3, potential, inv_root, boundary, second_out):
    hot = boundary_hot(boundary[...], own.shape[1])
    image = gathered_total(own[...], (a0, a1, a2, a3), hot, scaled[...], potential[...], inv_root[...])
    second = 2.0 * (image - CENTER * first[...].astype(F32)) * (1.0 / HALF) - start[...].astype(F32)
    second_out[...] = second.astype(BF16)


def body(states_in, kinetic, cell_scale, cell_nodes, boundary, potential, inv_mass_root):
    rows, owned = states_in.shape
    rim = boundary.shape[0]
    corners, cells = cell_nodes.shape
    height = (owned + len(OFFSETS) * rim) // (LANES // rows)
    per = LANES // corners
    block = jnp.kron(jnp.eye(per, dtype=BF16), kinetic)
    nodes_row = cell_nodes.T.reshape(cells // CHUNK, CHUNK * corners)
    edge = boundary[None, :]
    pot = potential[None, :]
    inv = inv_mass_root[None, :]
    field = jax.ShapeDtypeStruct((rows, owned), BF16)
    rim_shape = jax.ShapeDtypeStruct((rows, rim), BF16)

    def exchange(rim_values, scaled):
        ghosts = [from_behind(rim_values, "space", -offset) for offset in OFFSETS]
        own, *parts = call(
            cells_kernel,
            (jax.ShapeDtypeStruct((rows, owned), F32),) + (rim_shape,) * len(OFFSETS),
            scaled, *ghosts, cell_nodes, nodes_row, cell_scale, block,
            scratch=[pltpu.VMEM((LANES, height), BF16), pltpu.VMEM((height, LANES), F32)],
            specs=[VMEM] * 7 + [pl.BlockSpec(memory_space=pltpu.SMEM), VMEM],
        )
        return own, [from_behind(part, "space", offset) for part, offset in zip(parts, OFFSETS)]

    scaled, rim_values = call(pre_kernel, (field, rim_shape), states_in, inv, edge)
    own, arrived = exchange(rim_values, scaled)
    first, again, rim_values = call(
        mid_kernel, (field, field, rim_shape), states_in, scaled, own, *arrived, pot, inv, edge
    )
    own, arrived = exchange(rim_values, again)
    filtered = call(post_kernel, field, states_in, first, again, own, *arrived, pot, inv, edge)
    node_total = owned * lax.axis_size("space")
    regrouped = lax.all_to_all(filtered, "band", split_axis=1, concat_axis=0, tiled=True)
    partial_sum = lax.dot_general(regrouped, regrouped, NT, preferred_element_type=F32)
    reduced = lax.psum_scatter(partial_sum.astype(BF16), "band", scatter_dimension=0, tiled=True)
    mine = lax.psum(reduced.astype(F32), "space")
    return (filtered, mine / node_total)


def solution(mesh):
    in_specs = (
        P("band", "space"),
        P(),
        P("space"),
        P(None, "space"),
        P("space"),
        P("space"),
        P("space"),
    )
    out_specs = (P("band", "space"), P("band", None))
    return jax.shard_map(body, mesh=mesh, in_specs=in_specs, out_specs=out_specs, check_vma=False)
```

```python
import jax
import jax.numpy as jnp
from jax import lax
from jax.experimental import pallas as pl
from jax.experimental.pallas import tpu as pltpu
from jax.sharding import PartitionSpec as P

OFFSETS = (-2, -1, 1, 2)
CENTER = 0.5
HALF = 6.0
LANES = 256
CHUNK = 16
F32 = jnp.float32
BF16 = jnp.bfloat16
MESH = pl.DeviceIdType.MESH
NT = (((1,), (1,)), ((), ()))


def scaled_of(values, inv_root):
    return (inv_root * values.astype(F32)).astype(BF16)


def place(at, width, height, rows):
    return at // height * rows, at % height, min(width, height)


def apply_cells(scaled, ghosts, nodes, nodes_row, scale, block, table, total):
    rows, owned = scaled.shape
    rim = ghosts.shape[-1]
    height = table.shape[1]
    shift = height.bit_length() - 1
    corners = nodes.shape[0]
    step = CHUNK * corners
    for at in range(0, owned, height):
        row, col, width = place(at, owned, height, rows)
        table[row : row + rows, col : col + width] = scaled[:, at : at + width]
    for slot in range(len(OFFSETS)):
        row, col, width = place(owned + slot * rim, rim, height, rows)
        table[row : row + rows, col : col + width] = ghosts[slot]
    total[...] = jnp.zeros_like(total)
    part_lane = lax.broadcasted_iota(jnp.int32, (corners, 128), 1) // rows
    lane_b = lax.broadcasted_iota(jnp.int32, (corners, 128), 1).astype(F32).astype(BF16)
    high_count = height // 128

    def chunk(g, carry):
        base = g * CHUNK
        block_at = pl.multiple_of(base // 128 * 128, 128)
        ids = nodes[:, pl.ds(block_at, 128)]
        ids = pltpu.roll(ids, lax.rem(128 - lax.rem(base, 128), 128), axis=1)
        low = (ids & 127).astype(F32)
        high = ((ids >> 7) & (high_count - 1)).astype(F32)
        part = ids >> shift
        hots, masks = [], []
        for c in range(CHUNK):
            lo = jnp.broadcast_to(low[:, c : c + 1], (corners, 128)).astype(BF16)
            hi = jnp.broadcast_to(high[:, c : c + 1], (corners, 128)).astype(BF16)
            pt = jnp.broadcast_to(part[:, c : c + 1], (corners, 128))
            one = jnp.where(lo == lane_b, 1.0, 0.0).astype(BF16)
            hots.append(
                jnp.concatenate(
                    [jnp.where(hi == jnp.asarray(b, BF16), one, jnp.zeros_like(one)) for b in range(high_count)],
                    axis=1,
                )
            )
            masks.append(
                jnp.concatenate([pt == part_lane + k * (128 // rows) for k in range(LANES // 128)], axis=1)
            )
        hot = jnp.concatenate(hots, axis=0)
        found = lax.dot_general(hot, table[...], NT, preferred_element_type=F32)

        row = nodes_row[pl.ds(g, 1), :]
        low_row = jnp.broadcast_to((row & 127).astype(F32), (16, step)).astype(BF16)
        high_row = jnp.broadcast_to(((row >> 7) & (high_count - 1)).astype(F32), (16, step)).astype(BF16)
        sub = lax.broadcasted_iota(jnp.int32, (16, step), 0)
        ones_t = [
            jnp.where(low_row == (sub + s).astype(F32).astype(BF16), 1.0, 0.0).astype(BF16)
            for s in range(0, 128, 16)
        ]
        hots_t = []
        for b in range(high_count):
            here = high_row == jnp.asarray(b, BF16)
            hots_t += [jnp.where(here, one, jnp.zeros_like(one)) for one in ones_t]
        hot_t = jnp.concatenate(hots_t, axis=0)

        terms = []
        per = LANES // corners
        for q in range(0, CHUNK, per):
            picked = jnp.concatenate(
                [
                    jnp.where(masks[c], found[c * corners : (c + 1) * corners], 0.0).astype(BF16)
                    for c in range(q, q + per)
                ],
                axis=0,
            )
            term = jnp.dot(block[...], picked, preferred_element_type=F32)
            folded = term[:, :128]
            for k in range(128, LANES, 128):
                folded = folded + term[:, k : k + 128]
            spread = rows
            while spread < 128:
                folded = folded + pltpu.roll(folded, spread, axis=1)
                spread *= 2
            for c in range(q, q + per):
                mine = folded[(c - q) * corners : (c - q + 1) * corners] * scale[base + c]
                wide = jnp.concatenate([mine] * (LANES // 128), axis=1)
                terms.append(jnp.where(masks[c], wide, 0.0).astype(BF16))
        total[...] += jnp.dot(hot_t, jnp.concatenate(terms, axis=0), preferred_element_type=F32)
        return carry

    lax.fori_loop(0, nodes.shape[1] // CHUNK, chunk, 0)


def kernel(
    n_space, n_band,
    start, block, scale, nodes, nodes_row, edge, potential, inv_root,
    filtered, margin,
    hot, scaled, first, table, total, rims, ghosts, parts, back, quarters, gram, gram_in, gathered,
    rim_send, rim_recv, part_send, part_recv, quarter_send, quarter_recv, gram_send, gram_recv, row_send, row_recv,
):
    p, b = lax.axis_index("space"), lax.axis_index("band")
    space_at = [(lax.rem(p + k, n_space), b) for k in range(n_space)]
    band_at = [(p, lax.rem(b + k, n_band)) for k in range(n_band)]
    barrier = pltpu.get_barrier_semaphore()
    for device in space_at[1:] + band_at[1:]:
        pl.semaphore_signal(barrier, inc=1, device_id=device, device_id_type=MESH)

    def remote(src, dst, send, recv, device):
        copy = pltpu.make_async_remote_copy(
            src_ref=src, dst_ref=dst, send_sem=send, recv_sem=recv, device_id=device, device_id_type=MESH
        )
        copy.start()
        return copy

    rows, owned = start.shape
    rim = edge.shape[-1]
    height = table.shape[1]
    node_at = lax.broadcasted_iota(jnp.int32, (owned, rim), 0)
    hot[...] = jnp.where(node_at == edge[...], 1.0, 0.0).astype(BF16)

    def operate(turn, values):
        scaled[...] = scaled_of(values, inv_root[...])
        rims[turn] = jnp.dot(scaled[...], hot[...], preferred_element_type=F32).astype(BF16)
        if turn == 0:
            pl.semaphore_wait(barrier, n_space + n_band - 2)
        sent = [
            remote(
                rims.at[turn], ghosts.at[turn, slot], rim_send.at[turn, slot], rim_recv.at[turn, slot],
                space_at[-offset % n_space],
            )
            for slot, offset in enumerate(OFFSETS)
        ]
        for copy in sent:
            copy.wait()
        apply_cells(scaled, ghosts.at[turn], nodes, nodes_row, scale, block, table, total)
        sent = []
        for slot, offset in enumerate(OFFSETS):
            row, col, width = place(owned + slot * rim, rim, height, rows)
            parts[turn, slot] = total[col : col + width, row : row + rows].T.astype(BF16)
            sent.append(
                remote(
                    parts.at[turn, slot], back.at[turn, slot], part_send.at[turn, slot], part_recv.at[turn, slot],
                    space_at[offset % n_space],
                )
            )
        own = []
        for at in range(0, owned, height):
            row, col, width = place(at, owned, height, rows)
            own.append(total[col : col + width, row : row + rows].T)
        own = jnp.concatenate(own, axis=1) + potential[...] * scaled[...].astype(F32)
        for copy in sent:
            copy.wait()
        extra = sum(back[turn, slot].astype(F32) for slot in range(len(OFFSETS))).astype(BF16)
        added = lax.dot_general(extra, hot[...], NT, preferred_element_type=F32)
        return inv_root[...] * (own + added)

    image = operate(0, start[...])
    first[...] = ((image - CENTER * start[...].astype(F32)) / HALF).astype(BF16)
    image = operate(1, first[...])
    second = 2.0 * (image - CENTER * first[...].astype(F32)) / HALF - start[...].astype(F32)
    filtered[...] = second.astype(BF16)

    share = owned // n_band
    sent = []
    for k in range(1, n_band):
        at = pl.multiple_of(band_at[k][1] * share, share)
        sent.append(
            remote(
                filtered.at[:, pl.ds(at, share)], quarters.at[b], quarter_send.at[k], quarter_recv.at[k], band_at[k]
            )
        )
    quarters[b] = filtered[:, pl.ds(pl.multiple_of(b * share, share), share)]
    for copy in sent:
        copy.wait()
    states = quarters[...].reshape(n_band * rows, share)
    gram[...] = (
        lax.dot_general(states, states, NT, preferred_element_type=F32).astype(BF16).reshape(gram.shape)
    )
    sent = [
        remote(gram.at[band_at[k][1]], gram_in.at[b], gram_send.at[k], gram_recv.at[k], band_at[k])
        for k in range(1, n_band)
    ]
    gram_in[b] = gram[b]
    for copy in sent:
        copy.wait()
    gathered[p] = sum(gram_in[k].astype(F32) for k in range(n_band)).astype(BF16)
    sent = [
        remote(gathered.at[p], gathered.at[p], row_send.at[k], row_recv.at[k], space_at[k])
        for k in range(1, n_space)
    ]
    for copy in sent:
        copy.wait()
    margin[...] = sum(gathered[k].astype(F32) for k in range(n_space)) / (owned * n_space)


def body(n_space, n_band, states_in, kinetic, cell_scale, cell_nodes, boundary, potential, inv_mass_root):
    rows, owned = states_in.shape
    rim = boundary.shape[0]
    corners, cells = cell_nodes.shape
    slots = len(OFFSETS)
    height = (owned + slots * rim) // (LANES // rows)
    block = jnp.kron(jnp.eye(LANES // corners, dtype=BF16), kinetic)
    nodes_row = cell_nodes.T.reshape(cells // CHUNK, CHUNK * corners)
    vmem = pl.BlockSpec(memory_space=pltpu.VMEM)
    smem = pl.BlockSpec(memory_space=pltpu.SMEM)
    states = n_band * rows

    def run(*refs):
        kernel(n_space, n_band, *refs)

    return pl.pallas_call(
        run,
        out_shape=(
            jax.ShapeDtypeStruct((rows, owned), BF16),
            jax.ShapeDtypeStruct((rows, states), F32),
        ),
        in_specs=[vmem, vmem, smem] + [vmem] * 5,
        out_specs=(vmem, vmem),
        scratch_shapes=[
            pltpu.VMEM((owned, rim), BF16),
            pltpu.VMEM((rows, owned), BF16),
            pltpu.VMEM((rows, owned), BF16),
            pltpu.VMEM((LANES, height), BF16),
            pltpu.VMEM((height, LANES), F32),
            pltpu.VMEM((2, rows, rim), BF16),
            pltpu.VMEM((2, slots, rows, rim), BF16),
            pltpu.VMEM((2, slots, rows, rim), BF16),
            pltpu.VMEM((2, slots, rows, rim), BF16),
            pltpu.VMEM((n_band, rows, owned // n_band), BF16),
            pltpu.VMEM((n_band, rows, states), BF16),
            pltpu.VMEM((n_band, rows, states), BF16),
            pltpu.VMEM((n_space, rows, states), BF16),
        ]
        + [pltpu.SemaphoreType.DMA((2, slots))] * 4
        + [pltpu.SemaphoreType.DMA((n_band,))] * 4
        + [pltpu.SemaphoreType.DMA((n_space,))] * 2,
        compiler_params=pltpu.CompilerParams(
            collective_id=0, has_side_effects=True, vmem_limit_bytes=56 * 2**20
        ),
    )(
        states_in, block, cell_scale, cell_nodes, nodes_row,
        boundary[None, :], potential[None, :], inv_mass_root[None, :],
    )


def solution(mesh):
    n_space, n_band = mesh.shape["space"], mesh.shape["band"]
    in_specs = (
        P("band", "space"),
        P(),
        P("space"),
        P(None, "space"),
        P("space"),
        P("space"),
        P("space"),
    )
    out_specs = (P("band", "space"), P("band", None))

    def run(*args):
        return body(n_space, n_band, *args)

    return jax.shard_map(run, mesh=mesh, in_specs=in_specs, out_specs=out_specs, check_vma=False)
```

```python
import jax
import jax.numpy as jnp
from jax import lax
from jax.experimental import pallas as pl
from jax.experimental.pallas import tpu as pltpu
from jax.sharding import PartitionSpec as P

OFFSETS = (-2, -1, 1, 2)
CENTER = 0.5
HALF = 6.0
LANES = 256
CHUNK = 16
F32 = jnp.float32
BF16 = jnp.bfloat16
MESH = pl.DeviceIdType.MESH
NT = (((1,), (1,)), ((), ()))


def scaled_of(values, inv_root):
    return (inv_root * values.astype(F32)).astype(BF16)


def place(at, width, height, rows):
    return at // height * rows, at % height, min(width, height)


def apply_cells(scaled, ghosts, nodes, nodes_row, scale, block, table, turned, total):
    rows, owned = scaled.shape
    rim = ghosts.shape[-1]
    height = table.shape[1]
    shift = height.bit_length() - 1
    corners = nodes.shape[0]
    step = CHUNK * corners
    for at in range(0, owned, height):
        row, col, width = place(at, owned, height, rows)
        table[row : row + rows, col : col + width] = scaled[:, at : at + width]
    for slot in range(len(OFFSETS)):
        row, col, width = place(owned + slot * rim, rim, height, rows)
        table[row : row + rows, col : col + width] = ghosts[slot]
    turned[...] = table[...].astype(F32).T.astype(BF16)
    total[...] = jnp.zeros_like(total)
    part_lane = [
        ((lax.broadcasted_iota(jnp.int32, (corners, 128), 1) + k) // rows).astype(F32).astype(BF16)
        for k in range(0, LANES, 128)
    ]
    lane_b = lax.broadcasted_iota(jnp.int32, (corners, 128), 1).astype(F32).astype(BF16)
    high_count = height // 128

    def chunk(g, carry):
        base = g * CHUNK
        block_at = pl.multiple_of(base // 128 * 128, 128)
        ids = nodes[:, pl.ds(block_at, 128)]
        ids = pltpu.roll(ids, lax.rem(128 - lax.rem(base, 128), 128), axis=1)
        low = (ids & 127).astype(F32)
        high = ((ids >> 7) & (high_count - 1)).astype(F32)
        part = (ids >> shift).astype(F32)
        hots, masks = [], []
        for c in range(CHUNK):
            lo = jnp.broadcast_to(low[:, c : c + 1], (corners, 128)).astype(BF16)
            hi = jnp.broadcast_to(high[:, c : c + 1], (corners, 128)).astype(BF16)
            pt = jnp.broadcast_to(part[:, c : c + 1], (corners, 128)).astype(BF16)
            one = jnp.where(lo == lane_b, 1.0, 0.0).astype(BF16)
            hots.append(
                jnp.concatenate(
                    [jnp.where(hi == jnp.asarray(b, BF16), one, jnp.zeros_like(one)) for b in range(high_count)],
                    axis=1,
                )
            )
            masks.append(
                jnp.concatenate([jnp.where(pt == lanes, 1.0, 0.0).astype(BF16) for lanes in part_lane], axis=1)
            )
        hot = jnp.concatenate(hots, axis=0)
        found = jnp.dot(hot, turned[...], preferred_element_type=F32)

        row = nodes_row[pl.ds(g, 1), :]
        low_row = jnp.broadcast_to((row & 127).astype(F32), (16, step)).astype(BF16)
        high_row = jnp.broadcast_to(((row >> 7) & (high_count - 1)).astype(F32), (16, step)).astype(BF16)
        sub = lax.broadcasted_iota(jnp.int32, (16, step), 0)
        ones_t = [
            jnp.where(low_row == (sub + s).astype(F32).astype(BF16), 1.0, 0.0).astype(BF16)
            for s in range(0, 128, 16)
        ]
        hots_t = []
        for b in range(high_count):
            here = high_row == jnp.asarray(b, BF16)
            hots_t += [jnp.where(here, one, jnp.zeros_like(one)) for one in ones_t]
        hot_t = jnp.concatenate(hots_t, axis=0)

        terms = []
        per = LANES // corners
        for q in range(0, CHUNK, per):
            picked = jnp.concatenate(
                [
                    found[c * corners : (c + 1) * corners].astype(BF16) * masks[c]
                    for c in range(q, q + per)
                ],
                axis=0,
            )
            term = jnp.dot(block[...], picked, preferred_element_type=F32)
            folded = term[:, :128]
            for k in range(128, LANES, 128):
                folded = folded + term[:, k : k + 128]
            spread = rows
            while spread < 128:
                folded = folded + pltpu.roll(folded, spread, axis=1)
                spread *= 2
            for c in range(q, q + per):
                mine = (folded[(c - q) * corners : (c - q + 1) * corners] * scale[base + c]).astype(BF16)
                terms.append(jnp.concatenate([mine] * (LANES // 128), axis=1) * masks[c])
        total[...] += jnp.dot(hot_t, jnp.concatenate(terms, axis=0), preferred_element_type=F32)
        return carry

    lax.fori_loop(0, nodes.shape[1] // CHUNK, chunk, 0)


def kernel(
    n_space, n_band,
    start, kinetic, scale, nodes, nodes_row, edge, potential, inv_root,
    filtered, margin,
    hot, scaled, first, table, turned, total, block, rims, ghosts, parts, back, quarters, gram, gram_in, gathered,
    rim_send, rim_recv, part_send, part_recv, quarter_send, quarter_recv, gram_send, gram_recv, row_send, row_recv,
):
    p, b = lax.axis_index("space"), lax.axis_index("band")
    space_at = [(lax.rem(p + k, n_space), b) for k in range(n_space)]
    band_at = [(p, lax.rem(b + k, n_band)) for k in range(n_band)]
    barrier = pltpu.get_barrier_semaphore()
    for device in space_at[1:] + band_at[1:]:
        pl.semaphore_signal(barrier, inc=1, device_id=device, device_id_type=MESH)

    def remote(src, dst, send, recv, device):
        copy = pltpu.make_async_remote_copy(
            src_ref=src, dst_ref=dst, send_sem=send, recv_sem=recv, device_id=device, device_id_type=MESH
        )
        copy.start()
        return copy

    rows, owned = start.shape
    rim = edge.shape[-1]
    height = table.shape[1]
    corners = kinetic.shape[0]
    tiled = jnp.concatenate([kinetic[...].astype(F32)] * (LANES // corners), axis=0)
    tiled = jnp.concatenate([tiled] * (LANES // corners), axis=1)
    group = [lax.broadcasted_iota(jnp.int32, (LANES, LANES), axis) // corners for axis in (0, 1)]
    block[...] = jnp.where(group[0] == group[1], tiled, 0.0).astype(BF16)
    node_at = lax.broadcasted_iota(jnp.int32, (owned, rim), 0)
    hot[...] = jnp.where(node_at == edge[...], 1.0, 0.0).astype(BF16)

    def operate(turn, values):
        scaled[...] = scaled_of(values, inv_root[...])
        rims[turn] = jnp.dot(scaled[...], hot[...], preferred_element_type=F32).astype(BF16)
        if turn == 0:
            pl.semaphore_wait(barrier, n_space + n_band - 2)
        sent = [
            remote(
                rims.at[turn], ghosts.at[turn, slot], rim_send.at[turn, slot], rim_recv.at[turn, slot],
                space_at[-offset % n_space],
            )
            for slot, offset in enumerate(OFFSETS)
        ]
        for copy in sent:
            copy.wait()
        apply_cells(scaled, ghosts.at[turn], nodes, nodes_row, scale, block, table, turned, total)
        flipped = {}

        def piece(at, length):
            row, col, width = place(at, length, height, rows)
            column = row // 128 * 128
            if column not in flipped:
                flipped[column] = total[:, column : column + 128].T
            return flipped[column][row - column : row - column + rows, col : col + width]

        sent = []
        for slot, offset in enumerate(OFFSETS):
            parts[turn, slot] = piece(owned + slot * rim, rim).astype(BF16)
            sent.append(
                remote(
                    parts.at[turn, slot], back.at[turn, slot], part_send.at[turn, slot], part_recv.at[turn, slot],
                    space_at[offset % n_space],
                )
            )
        own = jnp.concatenate([piece(at, owned) for at in range(0, owned, height)], axis=1)
        own = own + potential[...] * scaled[...].astype(F32)
        for copy in sent:
            copy.wait()
        extra = sum(back[turn, slot].astype(F32) for slot in range(len(OFFSETS))).astype(BF16)
        added = lax.dot_general(extra, hot[...], NT, preferred_element_type=F32)
        return inv_root[...] * (own + added)

    image = operate(0, start[...])
    first[...] = ((image - CENTER * start[...].astype(F32)) / HALF).astype(BF16)
    image = operate(1, first[...])
    second = 2.0 * (image - CENTER * first[...].astype(F32)) / HALF - start[...].astype(F32)
    filtered[...] = second.astype(BF16)

    share = owned // n_band
    sent = []
    for k in range(1, n_band):
        at = pl.multiple_of(band_at[k][1] * share, share)
        sent.append(
            remote(
                filtered.at[:, pl.ds(at, share)], quarters.at[b], quarter_send.at[k], quarter_recv.at[k], band_at[k]
            )
        )
    quarters[b] = filtered[:, pl.ds(pl.multiple_of(b * share, share), share)]
    for copy in sent:
        copy.wait()
    states = quarters[...].reshape(n_band * rows, share)
    gram[...] = (
        lax.dot_general(states, states, NT, preferred_element_type=F32).astype(BF16).reshape(gram.shape)
    )
    sent = [
        remote(gram.at[band_at[k][1]], gram_in.at[b], gram_send.at[k], gram_recv.at[k], band_at[k])
        for k in range(1, n_band)
    ]
    gram_in[b] = gram[b]
    for copy in sent:
        copy.wait()
    gathered[p] = sum(gram_in[k].astype(F32) for k in range(n_band)).astype(BF16)
    sent = [
        remote(gathered.at[p], gathered.at[p], row_send.at[k], row_recv.at[k], space_at[k])
        for k in range(1, n_space)
    ]
    for copy in sent:
        copy.wait()
    margin[...] = sum(gathered[k].astype(F32) for k in range(n_space)) / (owned * n_space)


def body(n_space, n_band, states_in, kinetic, cell_scale, cell_nodes, boundary, potential, inv_mass_root):
    rows, owned = states_in.shape
    rim = boundary.shape[0]
    corners, cells = cell_nodes.shape
    slots = len(OFFSETS)
    height = (owned + slots * rim) // (LANES // rows)
    nodes_row = cell_nodes.T.reshape(cells // CHUNK, CHUNK * corners)
    vmem = pl.BlockSpec(memory_space=pltpu.VMEM)
    smem = pl.BlockSpec(memory_space=pltpu.SMEM)
    states = n_band * rows

    def run(*refs):
        kernel(n_space, n_band, *refs)

    return pl.pallas_call(
        run,
        out_shape=(
            jax.ShapeDtypeStruct((rows, owned), BF16),
            jax.ShapeDtypeStruct((rows, states), F32),
        ),
        in_specs=[vmem, vmem, smem] + [vmem] * 5,
        out_specs=(vmem, vmem),
        scratch_shapes=[
            pltpu.VMEM((owned, rim), BF16),
            pltpu.VMEM((rows, owned), BF16),
            pltpu.VMEM((rows, owned), BF16),
            pltpu.VMEM((LANES, height), BF16),
            pltpu.VMEM((height, LANES), BF16),
            pltpu.VMEM((height, LANES), F32),
            pltpu.VMEM((LANES, LANES), BF16),
            pltpu.VMEM((2, rows, rim), BF16),
            pltpu.VMEM((2, slots, rows, rim), BF16),
            pltpu.VMEM((2, slots, rows, rim), BF16),
            pltpu.VMEM((2, slots, rows, rim), BF16),
            pltpu.VMEM((n_band, rows, owned // n_band), BF16),
            pltpu.VMEM((n_band, rows, states), BF16),
            pltpu.VMEM((n_band, rows, states), BF16),
            pltpu.VMEM((n_space, rows, states), BF16),
        ]
        + [pltpu.SemaphoreType.DMA((2, slots))] * 4
        + [pltpu.SemaphoreType.DMA((n_band,))] * 4
        + [pltpu.SemaphoreType.DMA((n_space,))] * 2,
        compiler_params=pltpu.CompilerParams(
            collective_id=0, has_side_effects=True, vmem_limit_bytes=56 * 2**20
        ),
    )(
        states_in, kinetic, cell_scale, cell_nodes, nodes_row,
        boundary[None, :], potential[None, :], inv_mass_root[None, :],
    )


def solution(mesh):
    n_space, n_band = mesh.shape["space"], mesh.shape["band"]
    in_specs = (
        P("band", "space"),
        P(),
        P("space"),
        P(None, "space"),
        P("space"),
        P("space"),
        P("space"),
    )
    out_specs = (P("band", "space"), P("band", None))

    def run(*args):
        return body(n_space, n_band, *args)

    return jax.shard_map(run, mesh=mesh, in_specs=in_specs, out_specs=out_specs, check_vma=False)
```

```python
import jax
import jax.numpy as jnp
from jax import lax
from jax.experimental import pallas as pl
from jax.experimental.pallas import tpu as pltpu
from jax.sharding import PartitionSpec as P

OFFSETS = (-2, -1, 1, 2)
CENTER = 0.5
HALF = 6.0
LANES = 512
DEPTH = 256
CHUNK = 16
F32 = jnp.float32
BF16 = jnp.bfloat16
MESH = pl.DeviceIdType.MESH
NT = (((1,), (1,)), ((), ()))


def scaled_of(values, inv_root):
    return (inv_root * values.astype(F32)).astype(BF16)


def place(at, width, height, rows):
    return at // height * rows, at % height, min(width, height)


def apply_cells(scaled, ghosts, nodes, nodes_row, scale, block, table, turned, total):
    rows, owned = scaled.shape
    rim = ghosts.shape[-1]
    height = table.shape[1]
    shift = height.bit_length() - 1
    corners = nodes.shape[0]
    step = CHUNK * corners
    for at in range(0, owned, height):
        row, col, width = place(at, owned, height, rows)
        table[row : row + rows, col : col + width] = scaled[:, at : at + width]
    for slot in range(len(OFFSETS)):
        row, col, width = place(owned + slot * rim, rim, height, rows)
        table[row : row + rows, col : col + width] = ghosts[slot]
    turned[...] = table[...].astype(F32).T.astype(BF16)
    total[...] = jnp.zeros_like(total)
    part_lane = [
        ((lax.broadcasted_iota(jnp.int32, (corners, 128), 1) + k) // rows).astype(F32).astype(BF16)
        for k in range(0, LANES, 128)
    ]
    lane_b = lax.broadcasted_iota(jnp.int32, (corners, 128), 1).astype(F32).astype(BF16)
    high_count = height // 128

    def chunk(g, carry):
        base = g * CHUNK
        block_at = pl.multiple_of(base // 128 * 128, 128)
        ids = nodes[:, pl.ds(block_at, 128)]
        ids = pltpu.roll(ids, lax.rem(128 - lax.rem(base, 128), 128), axis=1)
        low = (ids & 127).astype(F32)
        high = ((ids >> 7) & (high_count - 1)).astype(F32)
        part = (ids >> shift).astype(F32)
        hots, masks = [], []
        for c in range(CHUNK):
            lo = jnp.broadcast_to(low[:, c : c + 1], (corners, 128)).astype(BF16)
            hi = jnp.broadcast_to(high[:, c : c + 1], (corners, 128)).astype(BF16)
            pt = jnp.broadcast_to(part[:, c : c + 1], (corners, 128)).astype(BF16)
            one = jnp.where(lo == lane_b, 1.0, 0.0).astype(BF16)
            hots.append(
                jnp.concatenate(
                    [jnp.where(hi == jnp.asarray(b, BF16), one, jnp.zeros_like(one)) for b in range(high_count)],
                    axis=1,
                )
            )
            masks.append(
                jnp.concatenate([jnp.where(pt == lanes, 1.0, 0.0).astype(BF16) for lanes in part_lane], axis=1)
            )
        hot = jnp.concatenate(hots, axis=0)
        found = jnp.dot(hot, turned[...], preferred_element_type=F32)

        row = nodes_row[pl.ds(g, 1), :]
        low_row = jnp.broadcast_to((row & 127).astype(F32), (16, step)).astype(BF16)
        high_row = jnp.broadcast_to(((row >> 7) & (high_count - 1)).astype(F32), (16, step)).astype(BF16)
        sub = lax.broadcasted_iota(jnp.int32, (16, step), 0)
        ones_t = [
            jnp.where(low_row == (sub + s).astype(F32).astype(BF16), 1.0, 0.0).astype(BF16)
            for s in range(0, 128, 16)
        ]
        hots_t = []
        for b in range(high_count):
            here = high_row == jnp.asarray(b, BF16)
            hots_t += [jnp.where(here, one, jnp.zeros_like(one)) for one in ones_t]
        hot_t = jnp.concatenate(hots_t, axis=0)

        per = DEPTH // corners
        picked = []
        for c in range(CHUNK):
            wide = found[c * corners : (c + 1) * corners].astype(BF16) * masks[c]
            picked.append(sum(wide[:, k : k + 128] for k in range(128, LANES, 128)) + wide[:, :128])
        left = lax.broadcasted_iota(jnp.int32, (corners, 128), 1) < rows
        pairs = [(at + cell, at + per + cell) for at in range(0, CHUNK, 2 * per) for cell in range(per)]
        tiles = []
        for one, two in pairs:
            first, other = picked[one].astype(F32), picked[two].astype(F32)
            crossed = pltpu.roll(jnp.where(left, other, first), rows, axis=1)
            tiles.append((jnp.where(left, first, other) + crossed).astype(BF16))
        columns = [jnp.concatenate(tiles[at : at + per], axis=0) for at in range(0, len(tiles), per)]
        term = jnp.dot(block[...], jnp.concatenate(columns, axis=1), preferred_element_type=F32)
        terms = [None] * CHUNK
        for k, (one, two) in enumerate(pairs):
            cell, column = k % per, k // per * 128
            tile = term[cell * corners : (cell + 1) * corners, column : column + 128]
            tile = tile * jnp.where(left, scale[base + one], scale[base + two])
            crossed = pltpu.roll(tile, rows, axis=1)
            for at, both in ((one, jnp.where(left, tile, crossed)), (two, jnp.where(left, crossed, tile))):
                terms[at] = jnp.concatenate([both.astype(BF16)] * (LANES // 128), axis=1) * masks[at]
        total[...] += jnp.dot(hot_t, jnp.concatenate(terms, axis=0), preferred_element_type=F32)
        return carry

    lax.fori_loop(0, nodes.shape[1] // CHUNK, chunk, 0)


def kernel(
    n_space, n_band,
    start, kinetic, scale, nodes, nodes_row, edge, potential, inv_root,
    filtered, margin,
    hot, scaled, first, table, turned, total, block, rims, ghosts, parts, back, quarters, gram, gram_in, gathered,
    rim_send, rim_recv, part_send, part_recv, quarter_send, quarter_recv, gram_send, gram_recv, row_send, row_recv,
):
    p, b = lax.axis_index("space"), lax.axis_index("band")
    space_at = [(lax.rem(p + k, n_space), b) for k in range(n_space)]
    band_at = [(p, lax.rem(b + k, n_band)) for k in range(n_band)]
    barrier = pltpu.get_barrier_semaphore()
    for device in space_at[1:] + band_at[1:]:
        pl.semaphore_signal(barrier, inc=1, device_id=device, device_id_type=MESH)

    def remote(src, dst, send, recv, device):
        copy = pltpu.make_async_remote_copy(
            src_ref=src, dst_ref=dst, send_sem=send, recv_sem=recv, device_id=device, device_id_type=MESH
        )
        copy.start()
        return copy

    rows, owned = start.shape
    rim = edge.shape[-1]
    height = table.shape[1]
    corners = kinetic.shape[0]
    tiled = jnp.concatenate([kinetic[...].astype(F32)] * (DEPTH // corners), axis=0)
    tiled = jnp.concatenate([tiled] * (DEPTH // corners), axis=1)
    group = [lax.broadcasted_iota(jnp.int32, (DEPTH, DEPTH), axis) // corners for axis in (0, 1)]
    block[...] = jnp.where(group[0] == group[1], tiled, 0.0).astype(BF16)
    node_at = lax.broadcasted_iota(jnp.int32, (owned, rim), 0)
    hot[...] = jnp.where(node_at == edge[...], 1.0, 0.0).astype(BF16)

    def operate(turn, values):
        scaled[...] = scaled_of(values, inv_root[...])
        rims[turn] = jnp.dot(scaled[...], hot[...], preferred_element_type=F32).astype(BF16)
        if turn == 0:
            pl.semaphore_wait(barrier, n_space + n_band - 2)
        sent = [
            remote(
                rims.at[turn], ghosts.at[turn, slot], rim_send.at[turn, slot], rim_recv.at[turn, slot],
                space_at[-offset % n_space],
            )
            for slot, offset in enumerate(OFFSETS)
        ]
        for copy in sent:
            copy.wait()
        apply_cells(scaled, ghosts.at[turn], nodes, nodes_row, scale, block, table, turned, total)
        flipped = {}

        def piece(at, length):
            row, col, width = place(at, length, height, rows)
            column = row // 128 * 128
            if column not in flipped:
                flipped[column] = total[:, column : column + 128].T
            return flipped[column][row - column : row - column + rows, col : col + width]

        sent = []
        for slot, offset in enumerate(OFFSETS):
            parts[turn, slot] = piece(owned + slot * rim, rim).astype(BF16)
            sent.append(
                remote(
                    parts.at[turn, slot], back.at[turn, slot], part_send.at[turn, slot], part_recv.at[turn, slot],
                    space_at[offset % n_space],
                )
            )
        own = jnp.concatenate([piece(at, owned) for at in range(0, owned, height)], axis=1)
        own = own + potential[...] * scaled[...].astype(F32)
        for copy in sent:
            copy.wait()
        extra = sum(back[turn, slot].astype(F32) for slot in range(len(OFFSETS))).astype(BF16)
        added = lax.dot_general(extra, hot[...], NT, preferred_element_type=F32)
        return inv_root[...] * (own + added)

    image = operate(0, start[...])
    first[...] = ((image - CENTER * start[...].astype(F32)) / HALF).astype(BF16)
    image = operate(1, first[...])
    second = 2.0 * (image - CENTER * first[...].astype(F32)) / HALF - start[...].astype(F32)
    filtered[...] = second.astype(BF16)

    share = owned // n_band
    sent = []
    for k in range(1, n_band):
        at = pl.multiple_of(band_at[k][1] * share, share)
        sent.append(
            remote(
                filtered.at[:, pl.ds(at, share)], quarters.at[b], quarter_send.at[k], quarter_recv.at[k], band_at[k]
            )
        )
    quarters[b] = filtered[:, pl.ds(pl.multiple_of(b * share, share), share)]
    for copy in sent:
        copy.wait()
    states = quarters[...].reshape(n_band * rows, share)
    gram[...] = (
        lax.dot_general(states, states, NT, preferred_element_type=F32).astype(BF16).reshape(gram.shape)
    )
    sent = [
        remote(gram.at[band_at[k][1]], gram_in.at[b], gram_send.at[k], gram_recv.at[k], band_at[k])
        for k in range(1, n_band)
    ]
    gram_in[b] = gram[b]
    for copy in sent:
        copy.wait()
    gathered[p] = sum(gram_in[k].astype(F32) for k in range(n_band)).astype(BF16)
    sent = [
        remote(gathered.at[p], gathered.at[p], row_send.at[k], row_recv.at[k], space_at[k])
        for k in range(1, n_space)
    ]
    for copy in sent:
        copy.wait()
    margin[...] = sum(gathered[k].astype(F32) for k in range(n_space)) / (owned * n_space)


def body(n_space, n_band, states_in, kinetic, cell_scale, cell_nodes, boundary, potential, inv_mass_root):
    rows, owned = states_in.shape
    rim = boundary.shape[0]
    corners, cells = cell_nodes.shape
    slots = len(OFFSETS)
    height = (owned + slots * rim) // (LANES // rows)
    nodes_row = cell_nodes.T.reshape(cells // CHUNK, CHUNK * corners)
    vmem = pl.BlockSpec(memory_space=pltpu.VMEM)
    smem = pl.BlockSpec(memory_space=pltpu.SMEM)
    states = n_band * rows

    def run(*refs):
        kernel(n_space, n_band, *refs)

    return pl.pallas_call(
        run,
        out_shape=(
            jax.ShapeDtypeStruct((rows, owned), BF16),
            jax.ShapeDtypeStruct((rows, states), F32),
        ),
        in_specs=[vmem, vmem, smem] + [vmem] * 5,
        out_specs=(vmem, vmem),
        scratch_shapes=[
            pltpu.VMEM((owned, rim), BF16),
            pltpu.VMEM((rows, owned), BF16),
            pltpu.VMEM((rows, owned), BF16),
            pltpu.VMEM((LANES, height), BF16),
            pltpu.VMEM((height, LANES), BF16),
            pltpu.VMEM((height, LANES), F32),
            pltpu.VMEM((DEPTH, DEPTH), BF16),
            pltpu.VMEM((2, rows, rim), BF16),
            pltpu.VMEM((2, slots, rows, rim), BF16),
            pltpu.VMEM((2, slots, rows, rim), BF16),
            pltpu.VMEM((2, slots, rows, rim), BF16),
            pltpu.VMEM((n_band, rows, owned // n_band), BF16),
            pltpu.VMEM((n_band, rows, states), BF16),
            pltpu.VMEM((n_band, rows, states), BF16),
            pltpu.VMEM((n_space, rows, states), BF16),
        ]
        + [pltpu.SemaphoreType.DMA((2, slots))] * 4
        + [pltpu.SemaphoreType.DMA((n_band,))] * 4
        + [pltpu.SemaphoreType.DMA((n_space,))] * 2,
        compiler_params=pltpu.CompilerParams(
            collective_id=0, has_side_effects=True, vmem_limit_bytes=56 * 2**20
        ),
    )(
        states_in, kinetic, cell_scale, cell_nodes, nodes_row,
        boundary[None, :], potential[None, :], inv_mass_root[None, :],
    )


def solution(mesh):
    n_space, n_band = mesh.shape["space"], mesh.shape["band"]
    in_specs = (
        P("band", "space"),
        P(),
        P("space"),
        P(None, "space"),
        P("space"),
        P("space"),
        P("space"),
    )
    out_specs = (P("band", "space"), P("band", None))

    def run(*args):
        return body(n_space, n_band, *args)

    return jax.shard_map(run, mesh=mesh, in_specs=in_specs, out_specs=out_specs, check_vma=False)
```

```python
import jax
import jax.numpy as jnp
from jax import lax
from jax.experimental import pallas as pl
from jax.experimental.pallas import tpu as pltpu
from jax.sharding import PartitionSpec as P

OFFSETS = (-2, -1, 1, 2)
CENTER = 0.5
HALF = 6.0
LANES = 512
DEPTH = 256
CHUNK = 16
F32 = jnp.float32
BF16 = jnp.bfloat16
MESH = pl.DeviceIdType.MESH
NT = (((1,), (1,)), ((), ()))


def scaled_of(values, inv_root):
    return (inv_root * values.astype(F32)).astype(BF16)


def place(at, width, height, rows):
    return at // height * rows, at % height, min(width, height)


def build_hots(nodes, nodes_row, hots, hots_t, part_of, height):
    shift = height.bit_length() - 1
    corners = nodes.shape[0]
    step = CHUNK * corners
    lane_b = lax.broadcasted_iota(jnp.int32, (corners, 128), 1).astype(F32).astype(BF16)
    sub = lax.broadcasted_iota(jnp.int32, (16, step), 0)
    high_count = height // 128

    def chunk(g, carry):
        base = g * CHUNK
        block_at = pl.multiple_of(base // 128 * 128, 128)
        ids = nodes[:, pl.ds(block_at, 128)]
        ids = pltpu.roll(ids, lax.rem(128 - lax.rem(base, 128), 128), axis=1)
        low = (ids & 127).astype(F32)
        high = ((ids >> 7) & (high_count - 1)).astype(F32)
        part = (ids >> shift).astype(F32)
        for c in range(CHUNK):
            at = pl.ds(c * corners, corners)
            lo = jnp.broadcast_to(low[:, c : c + 1], (corners, 128)).astype(BF16)
            hi = jnp.broadcast_to(high[:, c : c + 1], (corners, 128)).astype(BF16)
            part_of[g, at, :] = jnp.broadcast_to(part[:, c : c + 1], (corners, 128)).astype(BF16)
            one = jnp.where(lo == lane_b, 1.0, 0.0).astype(BF16)
            for b in range(high_count):
                hots[g, at, b * 128 : (b + 1) * 128] = jnp.where(hi == jnp.asarray(b, BF16), one, jnp.zeros_like(one))
        row = nodes_row[pl.ds(g, 1), :]
        low_row = jnp.broadcast_to((row & 127).astype(F32), (16, step)).astype(BF16)
        high_row = jnp.broadcast_to(((row >> 7) & (high_count - 1)).astype(F32), (16, step)).astype(BF16)
        here = [high_row == jnp.asarray(b, BF16) for b in range(high_count)]
        for s in range(0, 128, 16):
            one = jnp.where(low_row == (sub + s).astype(F32).astype(BF16), 1.0, 0.0).astype(BF16)
            for b in range(high_count):
                hots_t[g, b * 128 + s : b * 128 + s + 16, :] = jnp.where(here[b], one, jnp.zeros_like(one))
        return carry

    lax.fori_loop(0, hots.shape[0], chunk, 0)


def apply_cells(scaled, ghosts, hots, hots_t, part_of, scale, block, table, turned, spread, total):
    rows, owned = scaled.shape
    rim = ghosts.shape[-1]
    height = table.shape[1]
    corners = hots.shape[1] // CHUNK
    count = hots.shape[0]
    for at in range(0, owned, height):
        row, col, width = place(at, owned, height, rows)
        table[row : row + rows, col : col + width] = scaled[:, at : at + width]
    for slot in range(len(OFFSETS)):
        row, col, width = place(owned + slot * rim, rim, height, rows)
        table[row : row + rows, col : col + width] = ghosts[slot]
    turned[...] = table[...].astype(F32).T.astype(BF16)
    lane = lax.broadcasted_iota(jnp.int32, (corners, 128), 1)
    part_lane = [((lane + k) // rows).astype(F32).astype(BF16) for k in range(0, LANES, 128)]
    left = lane < rows
    per = DEPTH // corners
    pairs = [(at + cell, at + per + cell) for at in range(0, CHUNK, 2 * per) for cell in range(per)]

    def find(g):
        return jnp.dot(hots[g], turned[...], preferred_element_type=F32)

    def add(g):
        total[...] += jnp.dot(hots_t[g], spread[...], preferred_element_type=F32)

    def apply(g, found):
        base = g * CHUNK

        def mask(c):
            part = part_of[g, c * corners : (c + 1) * corners, :]
            return [jnp.where(part == lanes, 1.0, 0.0).astype(BF16) for lanes in part_lane]

        def pick(c):
            wide = found[c * corners : (c + 1) * corners].astype(BF16)
            return sum(wide[:, k * 128 : (k + 1) * 128] * m for k, m in enumerate(mask(c))).astype(F32)

        tiles = []
        for one, two in pairs:
            first, other = pick(one), pick(two)
            crossed = pltpu.roll(jnp.where(left, other, first), rows, axis=1)
            tiles.append((jnp.where(left, first, other) + crossed).astype(BF16))
        columns = [jnp.concatenate(tiles[at : at + per], axis=0) for at in range(0, len(tiles), per)]
        term = jnp.dot(block[...], jnp.concatenate(columns, axis=1), preferred_element_type=F32)
        for k, (one, two) in enumerate(pairs):
            cell, column = k % per, k // per * 128
            tile = term[cell * corners : (cell + 1) * corners, column : column + 128]
            tile = tile * jnp.where(left, scale[base + one], scale[base + two])
            crossed = pltpu.roll(tile, rows, axis=1)
            for at, both in ((one, jnp.where(left, tile, crossed)), (two, jnp.where(left, crossed, tile))):
                narrow = both.astype(BF16)
                for n, m in enumerate(mask(at)):
                    spread[at * corners : (at + 1) * corners, n * 128 : (n + 1) * 128] = narrow * m

    total[...] = jnp.zeros_like(total)
    apply(0, find(0))

    def chunk(g, carry):
        found = find(g)
        add(g - 1)
        apply(g, found)
        return carry

    lax.fori_loop(1, count, chunk, 0)
    add(count - 1)


def kernel(
    n_space, n_band,
    start, kinetic, scale, nodes, nodes_row, edge, potential, inv_root,
    filtered, margin,
    hot, scaled, first, table, turned, total, block, hots, hots_t, part_of, spread, rims, ghosts, parts, back, quarters, gram, gram_in, gathered,
    rim_send, rim_recv, part_send, part_recv, quarter_send, quarter_recv, gram_send, gram_recv, row_send, row_recv,
):
    p, b = lax.axis_index("space"), lax.axis_index("band")
    space_at = [(lax.rem(p + k, n_space), b) for k in range(n_space)]
    band_at = [(p, lax.rem(b + k, n_band)) for k in range(n_band)]
    barrier = pltpu.get_barrier_semaphore()
    for device in space_at[1:] + band_at[1:]:
        pl.semaphore_signal(barrier, inc=1, device_id=device, device_id_type=MESH)

    def remote(src, dst, send, recv, device):
        copy = pltpu.make_async_remote_copy(
            src_ref=src, dst_ref=dst, send_sem=send, recv_sem=recv, device_id=device, device_id_type=MESH
        )
        copy.start()
        return copy

    rows, owned = start.shape
    rim = edge.shape[-1]
    height = table.shape[1]
    corners = kinetic.shape[0]
    tiled = jnp.concatenate([kinetic[...].astype(F32)] * (DEPTH // corners), axis=0)
    tiled = jnp.concatenate([tiled] * (DEPTH // corners), axis=1)
    group = [lax.broadcasted_iota(jnp.int32, (DEPTH, DEPTH), axis) // corners for axis in (0, 1)]
    block[...] = jnp.where(group[0] == group[1], tiled, 0.0).astype(BF16)
    node_at = lax.broadcasted_iota(jnp.int32, (owned, rim), 0)
    hot[...] = jnp.where(node_at == edge[...], 1.0, 0.0).astype(BF16)

    def operate(turn, values):
        scaled[...] = scaled_of(values, inv_root[...])
        rims[turn] = jnp.dot(scaled[...], hot[...], preferred_element_type=F32).astype(BF16)
        if turn == 0:
            pl.semaphore_wait(barrier, n_space + n_band - 2)
        sent = [
            remote(
                rims.at[turn], ghosts.at[turn, slot], rim_send.at[turn, slot], rim_recv.at[turn, slot],
                space_at[-offset % n_space],
            )
            for slot, offset in enumerate(OFFSETS)
        ]
        if turn == 0:
            build_hots(nodes, nodes_row, hots, hots_t, part_of, height)
        for copy in sent:
            copy.wait()
        apply_cells(
            scaled, ghosts.at[turn], hots, hots_t, part_of, scale, block, table, turned, spread, total
        )
        flipped = {}

        def piece(at, length):
            row, col, width = place(at, length, height, rows)
            column = row // 128 * 128
            if column not in flipped:
                flipped[column] = total[:, column : column + 128].T
            return flipped[column][row - column : row - column + rows, col : col + width]

        sent = []
        for slot, offset in enumerate(OFFSETS):
            parts[turn, slot] = piece(owned + slot * rim, rim).astype(BF16)
            sent.append(
                remote(
                    parts.at[turn, slot], back.at[turn, slot], part_send.at[turn, slot], part_recv.at[turn, slot],
                    space_at[offset % n_space],
                )
            )
        own = jnp.concatenate([piece(at, owned) for at in range(0, owned, height)], axis=1)
        own = own + potential[...] * scaled[...].astype(F32)
        for copy in sent:
            copy.wait()
        extra = sum(back[turn, slot].astype(F32) for slot in range(len(OFFSETS))).astype(BF16)
        added = lax.dot_general(extra, hot[...], NT, preferred_element_type=F32)
        return inv_root[...] * (own + added)

    image = operate(0, start[...])
    first[...] = ((image - CENTER * start[...].astype(F32)) / HALF).astype(BF16)
    image = operate(1, first[...])
    second = 2.0 * (image - CENTER * first[...].astype(F32)) / HALF - start[...].astype(F32)
    filtered[...] = second.astype(BF16)

    share = owned // n_band
    sent = []
    for k in range(1, n_band):
        at = pl.multiple_of(band_at[k][1] * share, share)
        sent.append(
            remote(
                filtered.at[:, pl.ds(at, share)], quarters.at[b], quarter_send.at[k], quarter_recv.at[k], band_at[k]
            )
        )
    quarters[b] = filtered[:, pl.ds(pl.multiple_of(b * share, share), share)]
    for copy in sent:
        copy.wait()
    states = quarters[...].reshape(n_band * rows, share)
    gram[...] = (
        lax.dot_general(states, states, NT, preferred_element_type=F32).astype(BF16).reshape(gram.shape)
    )
    sent = [
        remote(gram.at[band_at[k][1]], gram_in.at[b], gram_send.at[k], gram_recv.at[k], band_at[k])
        for k in range(1, n_band)
    ]
    gram_in[b] = gram[b]
    for copy in sent:
        copy.wait()
    gathered[p] = sum(gram_in[k].astype(F32) for k in range(n_band)).astype(BF16)
    sent = [
        remote(gathered.at[p], gathered.at[p], row_send.at[k], row_recv.at[k], space_at[k])
        for k in range(1, n_space)
    ]
    for copy in sent:
        copy.wait()
    margin[...] = sum(gathered[k].astype(F32) for k in range(n_space)) / (owned * n_space)


def body(n_space, n_band, states_in, kinetic, cell_scale, cell_nodes, boundary, potential, inv_mass_root):
    rows, owned = states_in.shape
    rim = boundary.shape[0]
    corners, cells = cell_nodes.shape
    slots = len(OFFSETS)
    height = (owned + slots * rim) // (LANES // rows)
    count, step = cells // CHUNK, CHUNK * corners
    nodes_row = cell_nodes.T.reshape(count, step)
    vmem = pl.BlockSpec(memory_space=pltpu.VMEM)
    smem = pl.BlockSpec(memory_space=pltpu.SMEM)
    states = n_band * rows

    def run(*refs):
        kernel(n_space, n_band, *refs)

    return pl.pallas_call(
        run,
        out_shape=(
            jax.ShapeDtypeStruct((rows, owned), BF16),
            jax.ShapeDtypeStruct((rows, states), F32),
        ),
        in_specs=[vmem, vmem, smem] + [vmem] * 5,
        out_specs=(vmem, vmem),
        scratch_shapes=[
            pltpu.VMEM((owned, rim), BF16),
            pltpu.VMEM((rows, owned), BF16),
            pltpu.VMEM((rows, owned), BF16),
            pltpu.VMEM((LANES, height), BF16),
            pltpu.VMEM((height, LANES), BF16),
            pltpu.VMEM((height, LANES), F32),
            pltpu.VMEM((DEPTH, DEPTH), BF16),
            pltpu.VMEM((count, step, height), BF16),
            pltpu.VMEM((count, height, step), BF16),
            pltpu.VMEM((count, step, 128), BF16),
            pltpu.VMEM((step, LANES), BF16),
            pltpu.VMEM((2, rows, rim), BF16),
            pltpu.VMEM((2, slots, rows, rim), BF16),
            pltpu.VMEM((2, slots, rows, rim), BF16),
            pltpu.VMEM((2, slots, rows, rim), BF16),
            pltpu.VMEM((n_band, rows, owned // n_band), BF16),
            pltpu.VMEM((n_band, rows, states), BF16),
            pltpu.VMEM((n_band, rows, states), BF16),
            pltpu.VMEM((n_space, rows, states), BF16),
        ]
        + [pltpu.SemaphoreType.DMA((2, slots))] * 4
        + [pltpu.SemaphoreType.DMA((n_band,))] * 4
        + [pltpu.SemaphoreType.DMA((n_space,))] * 2,
        compiler_params=pltpu.CompilerParams(
            collective_id=0, has_side_effects=True, vmem_limit_bytes=56 * 2**20
        ),
    )(
        states_in, kinetic, cell_scale, cell_nodes, nodes_row,
        boundary[None, :], potential[None, :], inv_mass_root[None, :],
    )


def solution(mesh):
    n_space, n_band = mesh.shape["space"], mesh.shape["band"]
    in_specs = (
        P("band", "space"),
        P(),
        P("space"),
        P(None, "space"),
        P("space"),
        P("space"),
        P("space"),
    )
    out_specs = (P("band", "space"), P("band", None))

    def run(*args):
        return body(n_space, n_band, *args)

    return jax.shard_map(run, mesh=mesh, in_specs=in_specs, out_specs=out_specs, check_vma=False)
```

```python
import jax
import jax.numpy as jnp
from jax import lax
from jax.experimental import pallas as pl
from jax.experimental.pallas import tpu as pltpu
from jax.sharding import PartitionSpec as P

OFFSETS = (-2, -1, 1, 2)
CENTER = 0.5
HALF = 6.0
LANES = 512
DEPTH = 256
CHUNK = 16
F32 = jnp.float32
BF16 = jnp.bfloat16
MESH = pl.DeviceIdType.MESH
NT = (((1,), (1,)), ((), ()))


def scaled_of(values, inv_root):
    return (inv_root * values.astype(F32)).astype(BF16)


def place(at, width, height, rows):
    return at // height * rows, at % height, min(width, height)


def build_hots(nodes, nodes_row, hots, hots_t, part_of, height):
    shift = height.bit_length() - 1
    corners = nodes.shape[0]
    step = CHUNK * corners
    lane_b = lax.broadcasted_iota(jnp.int32, (corners, 128), 1).astype(F32).astype(BF16)
    sub = lax.broadcasted_iota(jnp.int32, (16, step), 0)
    high_count = height // 128

    def chunk(g, carry):
        base = g * CHUNK
        block_at = pl.multiple_of(base // 128 * 128, 128)
        ids = nodes[:, pl.ds(block_at, 128)]
        ids = pltpu.roll(ids, lax.rem(128 - lax.rem(base, 128), 128), axis=1)
        low = (ids & 127).astype(F32)
        high = ((ids >> 7) & (high_count - 1)).astype(F32)
        part = (ids >> shift).astype(F32)
        for c in range(CHUNK):
            at = pl.ds(c * corners, corners)
            lo = jnp.broadcast_to(low[:, c : c + 1], (corners, 128)).astype(BF16)
            hi = jnp.broadcast_to(high[:, c : c + 1], (corners, 128)).astype(BF16)
            part_of[g, at, :] = jnp.broadcast_to(part[:, c : c + 1], (corners, 128)).astype(BF16)
            one = jnp.where(lo == lane_b, 1.0, 0.0).astype(BF16)
            for b in range(high_count):
                hots[g, at, b * 128 : (b + 1) * 128] = jnp.where(hi == jnp.asarray(b, BF16), one, jnp.zeros_like(one))
        row = nodes_row[pl.ds(g, 1), :]
        low_row = jnp.broadcast_to((row & 127).astype(F32), (16, step)).astype(BF16)
        high_row = jnp.broadcast_to(((row >> 7) & (high_count - 1)).astype(F32), (16, step)).astype(BF16)
        here = [high_row == jnp.asarray(b, BF16) for b in range(high_count)]
        for s in range(0, 128, 16):
            one = jnp.where(low_row == (sub + s).astype(F32).astype(BF16), 1.0, 0.0).astype(BF16)
            for b in range(high_count):
                hots_t[g, b * 128 + s : b * 128 + s + 16, :] = jnp.where(here[b], one, jnp.zeros_like(one))
        return carry

    lax.fori_loop(0, hots.shape[0], chunk, 0)


class Cells:
    def __init__(self, hots, hots_t, part_of, scale, block, turned, middle, total, rows, own_lanes):
        self.hots, self.hots_t, self.part_of, self.scale, self.block = hots, hots_t, part_of, scale, block
        self.turned, self.middle, self.total, self.rows = turned, middle, total, rows
        self.own, self.ghost = (0, own_lanes), (own_lanes, LANES)
        self.corners = hots.shape[1] // CHUNK
        self.count = hots.shape[0]
        self.lane = lax.broadcasted_iota(jnp.int32, (self.corners, 128), 1)

    def mask(self, g, c, half):
        part = self.part_of[g, c * self.corners : (c + 1) * self.corners, :]
        for k in range(*half, 128):
            yield jnp.where(part == ((self.lane + k) // self.rows).astype(F32).astype(BF16), 1.0, 0.0).astype(BF16)

    def fill(self, half, pieces):
        stacked = jnp.concatenate(pieces, axis=0)
        self.turned[:, half[0] : half[1]] = stacked.astype(F32).T.astype(BF16)

    def find(self, g, half):
        return jnp.dot(self.hots[g], self.turned[:, half[0] : half[1]], preferred_element_type=F32)

    def pick(self, g, c, found, half):
        wide = found[c * self.corners : (c + 1) * self.corners].astype(BF16)
        return sum(wide[:, k * 128 : (k + 1) * 128] * m for k, m in enumerate(self.mask(g, c, half)))

    def gather_own(self):
        def chunk(g, carry):
            found = self.find(g, self.own)
            for c in range(CHUNK):
                self.middle[g, c * self.corners : (c + 1) * self.corners, :] = self.pick(g, c, found, self.own)
            return carry

        lax.fori_loop(0, self.count, chunk, 0)

    def add(self, g, half):
        spread = jnp.concatenate(
            [
                jnp.concatenate(
                    [
                        self.middle[g, c * self.corners : (c + 1) * self.corners, :] * m
                        for m in self.mask(g, c, half)
                    ],
                    axis=1,
                )
                for c in range(CHUNK)
            ],
            axis=0,
        )
        self.total[:, half[0] : half[1]] += jnp.dot(self.hots_t[g], spread, preferred_element_type=F32)

    def apply(self, g, found):
        corners, rows, base = self.corners, self.rows, g * CHUNK
        per = DEPTH // corners
        left = self.lane < rows
        pairs = [(at + cell, at + per + cell) for at in range(0, CHUNK, 2 * per) for cell in range(per)]

        def whole(c):
            earlier = self.middle[g, c * corners : (c + 1) * corners, :]
            return (earlier + self.pick(g, c, found, self.ghost)).astype(F32)

        tiles = []
        for one, two in pairs:
            here, other = whole(one), whole(two)
            crossed = pltpu.roll(jnp.where(left, other, here), rows, axis=1)
            tiles.append((jnp.where(left, here, other) + crossed).astype(BF16))
        columns = [jnp.concatenate(tiles[at : at + per], axis=0) for at in range(0, len(tiles), per)]
        term = jnp.dot(self.block[...], jnp.concatenate(columns, axis=1), preferred_element_type=F32)
        for k, (one, two) in enumerate(pairs):
            cell, column = k % per, k // per * 128
            tile = term[cell * corners : (cell + 1) * corners, column : column + 128]
            tile = tile * jnp.where(left, self.scale[base + one], self.scale[base + two])
            crossed = pltpu.roll(tile, rows, axis=1)
            for at, both in ((one, jnp.where(left, tile, crossed)), (two, jnp.where(left, crossed, tile))):
                self.middle[g, at * corners : (at + 1) * corners, :] = both.astype(BF16)

    def gather_ghosts_and_apply(self):
        self.total[...] = jnp.zeros_like(self.total)
        self.apply(0, self.find(0, self.ghost))

        def chunk(g, carry):
            found = self.find(g, self.ghost)
            self.add(g - 1, self.ghost)
            self.apply(g, found)
            return carry

        lax.fori_loop(1, self.count, chunk, 0)
        self.add(self.count - 1, self.ghost)

    def add_own(self):
        def chunk(g, carry):
            self.add(g, self.own)
            return carry

        lax.fori_loop(0, self.count, chunk, 0)


def kernel(
    n_space, n_band,
    start, kinetic, scale, nodes, nodes_row, edge, potential, inv_root,
    filtered, margin,
    hot, scaled, first, turned, total, block, hots, hots_t, part_of, middle, rims, ghosts, parts, back, quarters, gram, gram_in, gathered,
    rim_send, rim_recv, part_send, part_recv, quarter_send, quarter_recv, gram_send, gram_recv, row_send, row_recv,
):
    p, b = lax.axis_index("space"), lax.axis_index("band")
    space_at = [(lax.rem(p + k, n_space), b) for k in range(n_space)]
    band_at = [(p, lax.rem(b + k, n_band)) for k in range(n_band)]
    barrier = pltpu.get_barrier_semaphore()
    for device in space_at[1:] + band_at[1:]:
        pl.semaphore_signal(barrier, inc=1, device_id=device, device_id_type=MESH)

    def remote(src, dst, send, recv, device):
        copy = pltpu.make_async_remote_copy(
            src_ref=src, dst_ref=dst, send_sem=send, recv_sem=recv, device_id=device, device_id_type=MESH
        )
        copy.start()
        return copy

    rows, owned = start.shape
    rim = edge.shape[-1]
    height = turned.shape[0]
    cells = Cells(
        hots, hots_t, part_of, scale, block, turned, middle, total, rows, owned // height * rows
    )
    corners = kinetic.shape[0]
    tiled = jnp.concatenate([kinetic[...].astype(F32)] * (DEPTH // corners), axis=0)
    tiled = jnp.concatenate([tiled] * (DEPTH // corners), axis=1)
    group = [lax.broadcasted_iota(jnp.int32, (DEPTH, DEPTH), axis) // corners for axis in (0, 1)]
    block[...] = jnp.where(group[0] == group[1], tiled, 0.0).astype(BF16)
    node_at = lax.broadcasted_iota(jnp.int32, (owned, rim), 0)
    hot[...] = jnp.where(node_at == edge[...], 1.0, 0.0).astype(BF16)

    def operate(turn, values):
        scaled[...] = scaled_of(values, inv_root[...])
        rims[turn] = jnp.dot(scaled[...], hot[...], preferred_element_type=F32).astype(BF16)
        if turn == 0:
            pl.semaphore_wait(barrier, n_space + n_band - 2)
        sent = [
            remote(
                rims.at[turn], ghosts.at[turn, slot], rim_send.at[turn, slot], rim_recv.at[turn, slot],
                space_at[-offset % n_space],
            )
            for slot, offset in enumerate(OFFSETS)
        ]
        if turn == 0:
            build_hots(nodes, nodes_row, hots, hots_t, part_of, height)
        cells.fill(cells.own, [scaled[:, at : at + height] for at in range(0, owned, height)])
        cells.gather_own()
        for copy in sent:
            copy.wait()
        joined = jnp.concatenate([ghosts[turn, slot] for slot in range(len(OFFSETS))], axis=1)
        cells.fill(cells.ghost, [joined[:, at : at + height] for at in range(0, joined.shape[1], height)])
        cells.gather_ghosts_and_apply()
        flipped = {}

        def piece(at, length):
            row, col, width = place(at, length, height, rows)
            column = row // 128 * 128
            if column not in flipped:
                flipped[column] = total[:, column : column + 128].T
            return flipped[column][row - column : row - column + rows, col : col + width]

        sent = []
        for slot, offset in enumerate(OFFSETS):
            parts[turn, slot] = piece(owned + slot * rim, rim).astype(BF16)
            sent.append(
                remote(
                    parts.at[turn, slot], back.at[turn, slot], part_send.at[turn, slot], part_recv.at[turn, slot],
                    space_at[offset % n_space],
                )
            )
        cells.add_own()
        own = jnp.concatenate([piece(at, owned) for at in range(0, owned, height)], axis=1)
        own = own + potential[...] * scaled[...].astype(F32)
        for copy in sent:
            copy.wait()
        extra = sum(back[turn, slot].astype(F32) for slot in range(len(OFFSETS))).astype(BF16)
        added = lax.dot_general(extra, hot[...], NT, preferred_element_type=F32)
        return inv_root[...] * (own + added)

    image = operate(0, start[...])
    first[...] = ((image - CENTER * start[...].astype(F32)) / HALF).astype(BF16)
    image = operate(1, first[...])
    second = 2.0 * (image - CENTER * first[...].astype(F32)) / HALF - start[...].astype(F32)
    filtered[...] = second.astype(BF16)

    share = owned // n_band
    sent = []
    for k in range(1, n_band):
        at = pl.multiple_of(band_at[k][1] * share, share)
        sent.append(
            remote(
                filtered.at[:, pl.ds(at, share)], quarters.at[b], quarter_send.at[k], quarter_recv.at[k], band_at[k]
            )
        )
    quarters[b] = filtered[:, pl.ds(pl.multiple_of(b * share, share), share)]
    for copy in sent:
        copy.wait()
    states = quarters[...].reshape(n_band * rows, share)
    gram[...] = (
        lax.dot_general(states, states, NT, preferred_element_type=F32).astype(BF16).reshape(gram.shape)
    )
    sent = [
        remote(gram.at[band_at[k][1]], gram_in.at[b], gram_send.at[k], gram_recv.at[k], band_at[k])
        for k in range(1, n_band)
    ]
    gram_in[b] = gram[b]
    for copy in sent:
        copy.wait()
    gathered[p] = sum(gram_in[k].astype(F32) for k in range(n_band)).astype(BF16)
    sent = [
        remote(gathered.at[p], gathered.at[p], row_send.at[k], row_recv.at[k], space_at[k])
        for k in range(1, n_space)
    ]
    for copy in sent:
        copy.wait()
    margin[...] = sum(gathered[k].astype(F32) for k in range(n_space)) / (owned * n_space)


def body(n_space, n_band, states_in, kinetic, cell_scale, cell_nodes, boundary, potential, inv_mass_root):
    rows, owned = states_in.shape
    rim = boundary.shape[0]
    corners, cells = cell_nodes.shape
    slots = len(OFFSETS)
    height = (owned + slots * rim) // (LANES // rows)
    count, step = cells // CHUNK, CHUNK * corners
    nodes_row = cell_nodes.T.reshape(count, step)
    vmem = pl.BlockSpec(memory_space=pltpu.VMEM)
    smem = pl.BlockSpec(memory_space=pltpu.SMEM)
    states = n_band * rows

    def run(*refs):
        kernel(n_space, n_band, *refs)

    return pl.pallas_call(
        run,
        out_shape=(
            jax.ShapeDtypeStruct((rows, owned), BF16),
            jax.ShapeDtypeStruct((rows, states), F32),
        ),
        in_specs=[vmem, vmem, smem] + [vmem] * 5,
        out_specs=(vmem, vmem),
        scratch_shapes=[
            pltpu.VMEM((owned, rim), BF16),
            pltpu.VMEM((rows, owned), BF16),
            pltpu.VMEM((rows, owned), BF16),
            pltpu.VMEM((height, LANES), BF16),
            pltpu.VMEM((height, LANES), F32),
            pltpu.VMEM((DEPTH, DEPTH), BF16),
            pltpu.VMEM((count, step, height), BF16),
            pltpu.VMEM((count, height, step), BF16),
            pltpu.VMEM((count, step, 128), BF16),
            pltpu.VMEM((count, step, 128), BF16),
            pltpu.VMEM((2, rows, rim), BF16),
            pltpu.VMEM((2, slots, rows, rim), BF16),
            pltpu.VMEM((2, slots, rows, rim), BF16),
            pltpu.VMEM((2, slots, rows, rim), BF16),
            pltpu.VMEM((n_band, rows, owned // n_band), BF16),
            pltpu.VMEM((n_band, rows, states), BF16),
            pltpu.VMEM((n_band, rows, states), BF16),
            pltpu.VMEM((n_space, rows, states), BF16),
        ]
        + [pltpu.SemaphoreType.DMA((2, slots))] * 4
        + [pltpu.SemaphoreType.DMA((n_band,))] * 4
        + [pltpu.SemaphoreType.DMA((n_space,))] * 2,
        compiler_params=pltpu.CompilerParams(
            collective_id=0, has_side_effects=True, vmem_limit_bytes=58 * 2**20
        ),
    )(
        states_in, kinetic, cell_scale, cell_nodes, nodes_row,
        boundary[None, :], potential[None, :], inv_mass_root[None, :],
    )


def solution(mesh):
    n_space, n_band = mesh.shape["space"], mesh.shape["band"]
    in_specs = (
        P("band", "space"),
        P(),
        P("space"),
        P(None, "space"),
        P("space"),
        P("space"),
        P("space"),
    )
    out_specs = (P("band", "space"), P("band", None))

    def run(*args):
        return body(n_space, n_band, *args)

    return jax.shard_map(run, mesh=mesh, in_specs=in_specs, out_specs=out_specs, check_vma=False)
```
